256 devices in a mesh: rep: 8 (over y, core), shard: 32 (over z, x).
Axes of the slice: x: 4, y: 4, z: 8, core: 2. Of those that a mesh axis runs over, the one named last changes fastest.
Arguments:
- gradients: bfloat16 [8, 8192, 8192], P('rep', 'shard')
- owner_table: int32 [16, 16], replicated, may hold values from 0 to 15, each once within a row
- left_stats: float32 [8, 32, 1, 512, 512], P('rep', 'shard'), may hold values from -6 to 6
- right_stats: float32 [8, 32, 1, 512, 512], P('rep', 'shard'), may hold values from -6 to 6
- left_root: bfloat16 [8, 32, 1, 512, 512], P('rep', 'shard'), as said below
- right_root: bfloat16 [8, 32, 1, 512, 512], P('rep', 'shard'), as said below
Outputs:
- new_left: float32 [8, 32, 1, 512, 512], P('rep', 'shard')
- new_right: float32 [8, 32, 1, 512, 512], P('rep', 'shard')
- update: bfloat16 [8192, 8192], P('shard', 'rep')
The draws below stay inside these ranges and needn't reach their ends.
Inputs may be any that keep to these rules, and one draw needn't show every extreme that they name: Each row of owner_table is a permutation of 0 to 15. `left_root`: every matrix is symmetric. `right_root`: every matrix is symmetric.
All inputs are finite; a program needn't handle non-finite values.
Results may differ from the reference program's by a relative error of at most 0.025.
Values may be sent and summed in bfloat16 or wider, within the bound.
A program may use at most 64 MiB of HBM per device.

```python
import math
import jax
import jax.numpy as jnp
from jax import lax

D = 8192
BLOCK = 512
REPLICAS = 8
SHARDS = 32
ROWS = 8192
COLBLOCKS = 16
OWNED = 1
N_REP = 8
N_SHARD = 32


def shared_patterns(key):
    row_key = jax.random.fold_in(key, 101)
    col_key = jax.random.fold_in(key, 102)
    row_pattern = jnp.exp(jax.random.uniform(row_key, (BLOCK,), jnp.float32, 0.0, math.log(10.0)))
    col_pattern = jnp.exp(jax.random.uniform(col_key, (BLOCK,), jnp.float32, 0.0, math.log(10.0)))
    return (row_pattern, col_pattern)


def draw_gradients(key, part):
    row_pattern, col_pattern = shared_patterns(key)
    key = jax.random.fold_in(key, 11)
    subkeys = jax.random.split(key, 3)
    rising = 1.0 + 2.0 * jnp.arange(ROWS, dtype=jnp.float32) / ROWS
    row_jitter = jax.random.uniform(subkeys[0], (ROWS,), jnp.float32, 1.0, 1.5)
    col_jitter = jax.random.uniform(subkeys[1], (D,), jnp.float32, 1.0, 1.5)
    row_scale = jnp.tile(row_pattern, ROWS // BLOCK) * row_jitter * rising
    col_scale = jnp.tile(col_pattern, COLBLOCKS) * col_jitter
    values = jax.random.normal(subkeys[2], (REPLICAS, ROWS, D), jnp.float32) + 1.0 / math.sqrt(REPLICAS)
    factor = 0.004
    scaled = values * (factor * row_scale)[None, :, None] * col_scale[None, None, :]
    return scaled.astype(jnp.bfloat16)


def root_matrix(key, pattern, spread):
    subkeys = jax.random.split(key, 3)
    values = jax.random.normal(subkeys[0], (REPLICAS, SHARDS, OWNED, BLOCK, BLOCK), jnp.float32)
    symmetric = (values + jnp.swapaxes(values, -1, -2)) * (spread / math.sqrt(2.0 * BLOCK))
    diagonal_base = jax.random.uniform(subkeys[1], (REPLICAS, SHARDS, OWNED, BLOCK, 1), jnp.float32, 0.8, 1.6)
    diagonal = diagonal_base * (1.0 / jnp.sqrt(pattern))[:, None]
    identity = (jnp.arange(BLOCK)[:, None] == jnp.arange(BLOCK)[None, :]).astype(jnp.float32)
    weight = pattern / math.sqrt(99.0 / (2.0 * math.log(10.0)))
    coherent = 0.35 * weight[:, None] * weight[None, :] / BLOCK
    slot_scale = jnp.exp(jax.random.uniform(subkeys[2], (REPLICAS, SHARDS, OWNED, 1, 1), jnp.float32, -1.0, 1.0))
    return ((symmetric + identity * diagonal - coherent) * slot_scale).astype(jnp.bfloat16)


def draw_left_root(key, part):
    row_pattern, col_pattern = shared_patterns(key)
    key = jax.random.fold_in(key, 23)
    return root_matrix(key, row_pattern, 0.25)


def draw_right_root(key, part):
    row_pattern, col_pattern = shared_patterns(key)
    key = jax.random.fold_in(key, 37)
    return root_matrix(key, col_pattern, 0.25)


def steps_of(stream_key, extent, pieces, least, top_value):
    factor_of = 1.0
    for position, blocks in pieces:
        draws = jax.random.uniform(jax.random.fold_in(jax.random.fold_in(stream_key, 6), position), (blocks,), jnp.float32, least / len(pieces), top_value / len(pieces))
        factor_of = factor_of * jnp.repeat(jnp.exp(draws), extent[position] // blocks).reshape((-1,) + (1,) * (len(extent) - 1 - position))
    return factor_of


def centred(key, shape, deviation, most, pieces=(), kind=jnp.bfloat16):
    factor_of = steps_of(key, shape, pieces, -0.22, 0.18) if pieces else 1.0
    result = jax.random.normal(key, shape, jnp.float32) * deviation * factor_of
    return jnp.minimum(jnp.maximum(result, -most), most).astype(kind)


def setup_inputs(seed: int = 0) -> dict:
    streams_of = jax.random.split(jax.random.key(seed), 7)
    gradients = draw_gradients(jax.random.fold_in(streams_of[6], 71), 0)
    owner_table = jax.vmap(lambda own: jax.random.permutation(own, COLBLOCKS))(jax.random.split(streams_of[1], (ROWS // BLOCK))).reshape((ROWS // BLOCK, COLBLOCKS)).astype(jnp.int32)
    left_stats = centred(streams_of[2], (REPLICAS, SHARDS, OWNED, BLOCK, BLOCK), 1.0, 6.0, ((0, 8), (1, 32)), jnp.float32)
    right_stats = centred(streams_of[3], (REPLICAS, SHARDS, OWNED, BLOCK, BLOCK), 1.0, 6.0, ((0, 8), (1, 32)), jnp.float32)
    left_root = draw_left_root(jax.random.fold_in(streams_of[6], 71), 0)
    right_root = draw_right_root(jax.random.fold_in(streams_of[6], 71), 0)
    return {"gradients": gradients, "owner_table": owner_table, "left_stats": left_stats, "right_stats": right_stats, "left_root": left_root, "right_root": right_root}


def one_block(items):
    grad_block, left, right, left_factor, right_factor = items
    left_gram = jnp.dot(grad_block, grad_block.T, preferred_element_type=jnp.float32)
    right_gram = jnp.dot(grad_block.T, grad_block, preferred_element_type=jnp.float32)
    left_next = 0.95 * left + 0.05 * left_gram
    right_next = 0.95 * right + 0.05 * right_gram
    half_product = jnp.dot(grad_block, right_factor, preferred_element_type=jnp.float32).astype(jnp.bfloat16)
    precond = jnp.dot(left_factor, half_product, preferred_element_type=jnp.float32).astype(jnp.bfloat16)
    return (left_next, right_next, precond)

def reference(gradients, owner_table, left_stats, right_stats, left_root, right_root):
    grad = lax.optimization_barrier(jnp.sum(gradients.astype(jnp.float32), axis=0)).astype(jnp.bfloat16)
    block_rows = ROWS // BLOCK
    blocks = grad.reshape(block_rows, BLOCK, COLBLOCKS, BLOCK).transpose(0, 2, 1, 3)
    positions = jnp.arange(COLBLOCKS, dtype=jnp.int32)
    matches = owner_table[:, :, None] == positions[None, None, :]
    inverse = lax.optimization_barrier(jnp.sum(jnp.where(matches, positions[None, :, None], 0), axis=1)).astype(jnp.int32)
    replica_ids = jnp.arange(N_REP, dtype=jnp.int32)[:, None, None]
    shard_ids = jnp.arange(N_SHARD, dtype=jnp.int32)[None, :, None]
    slot_ids = jnp.arange(OWNED, dtype=jnp.int32)[None, None, :]
    values = (replica_ids * 2 + shard_ids % 2) * OWNED + slot_ids
    row_full = jnp.broadcast_to(shard_ids // 2, values.shape).astype(jnp.int32)
    column_ids = inverse[row_full, values]
    slot_blocks = blocks[row_full, column_ids]
    count = N_REP * N_SHARD * OWNED
    flat = (slot_blocks.reshape(count, BLOCK, BLOCK), left_stats.reshape(count, BLOCK, BLOCK), right_stats.reshape(count, BLOCK, BLOCK), left_root.reshape(count, BLOCK, BLOCK), right_root.reshape(count, BLOCK, BLOCK))
    left_next, right_next, precond = lax.map(one_block, flat)
    new_left = left_next.reshape(left_stats.shape)
    new_right = right_next.reshape(right_stats.shape)
    pre_slots = precond.reshape(N_REP, N_SHARD, OWNED, BLOCK, BLOCK)
    owner_rep = owner_table // OWNED // 2
    owner_parity = owner_table // OWNED % 2
    owner_slot = owner_table % OWNED
    shard_of = 2 * jnp.arange(block_rows, dtype=jnp.int32)[:, None] + owner_parity
    pre_blocks = pre_slots[owner_rep, shard_of, owner_slot]
    pre_full = pre_blocks.transpose(0, 2, 1, 3).reshape(ROWS, D)
    grad_square = jnp.sum(jnp.square(grad.astype(jnp.float32)))
    pre_square = jnp.sum(jnp.square(pre_full.astype(jnp.float32)))
    ratio = jnp.sqrt(grad_square + 1e-06) / jnp.sqrt(pre_square + 1e-06)
    update = (pre_full.astype(jnp.float32) * ratio).astype(jnp.bfloat16)
    return (new_left, new_right, update)
```

```python
import jax
import jax.numpy as jnp
from jax import lax
from jax.experimental import pallas as pl
from jax.experimental.pallas import tpu as pltpu
from jax.sharding import PartitionSpec as P

MESH = pl.DeviceIdType.MESH
F32 = jnp.float32
BF16 = jnp.bfloat16
REP = 8
YS = 4
XS = 4
ZS = 8
BLK = 512
HALF = 256
PART = 128
PIECE = 16
ORDER = ((2, 0), (1, 0), (3, 0), (0, 0), (2, 1), (1, 1), (3, 1), (0, 1))


def remote(src, dst, send, recv, rep, shard):
    return pltpu.make_async_remote_copy(
        src_ref=src, dst_ref=dst, send_sem=send, recv_sem=recv, device_id=(rep, shard), device_id_type=MESH
    )


def rows(start, size):
    return pl.ds(pl.multiple_of(start, size), size)


def squares(ref):
    def step(m, total):
        value = ref[rows(m * 32, 32), :].astype(F32)
        value = value * value
        for a in range(4):
            for b in range(4):
                total = total + value[8 * a : 8 * a + 8, 128 * b : 128 * b + 128]
        return total

    return lax.fori_loop(0, BLK // 32, step, jnp.zeros((8, 128), F32))


def kernel(
    grads, table, lstat, rstat, lroot, rroot, new_left, new_right, update,
    g, tab, inv, ds, dr, ys, yr, xs, blk, lst, rst, lrt, rrt, hp, pre, mid0, mid1, sb, col, out, zb, xb, rb,
    ld, ds_s, ds_r, y_s, y_r, x_s, x_r, a_s, a_r, b_s, b_r, z_s, z_r, v_s, v_r, r_s, r_r, o_s,
):
    r = lax.axis_index("rep")
    s = lax.axis_index("shard")
    y, c = r // 2, lax.rem(r, 2)
    p = lax.rem(s, 2)
    z, x = s // XS, lax.rem(s, XS)
    pair = s + 1 - 2 * p
    sibling = r + 1 - 2 * c

    def rep_at(k):
        return lax.rem(r + k, REP)

    def x_at(k):
        return z * XS + lax.rem(x + k, XS)

    def z_at(k):
        return lax.rem(z + k, ZS) * XS + x

    barrier = pltpu.get_barrier_semaphore()

    def greet(rep, shard):
        pl.semaphore_signal(barrier, inc=1, device_id=(rep, shard), device_id_type=MESH)

    for k in range(1, REP):
        greet(rep_at(k), s)
        greet(rep_at(k), pair)
    for k in range(1, ZS):
        greet(r, z_at(k))
    for k in range(1, XS):
        greet(r, x_at(k))

    get_table = pltpu.make_async_copy(table, tab, ld.at[16])
    get_table.start()
    loads = [
        pltpu.make_async_copy(grads.at[0, :, pl.ds(BLK * j, BLK)], g.at[j], ld.at[j]) for j in range(16)
    ]
    for copy in loads:
        copy.start()
    late = [
        pltpu.make_async_copy(src.at[0, 0, 0], dst, ld.at[17 + n])
        for n, (src, dst) in enumerate(((rroot, rrt), (lroot, lrt), (lstat, lst), (rstat, rst)))
    ]
    for copy in late:
        copy.start()

    get_table.wait()
    owners = [tab[s // 2, j] for j in range(16)]

    def invert(v, carry):
        place = jnp.int32(0)
        for j in range(1, 16):
            place = jnp.where(owners[j] == v, j, place)
        inv[v] = place
        return carry

    lax.fori_loop(0, 16, invert, 0)

    def place_of(delta, t, core):
        return inv[4 * lax.rem(y + delta, YS) + 2 * core + (p if t else 1 - p)]

    mine = [place_of(delta, t, c) for delta, t in ORDER]
    theirs = [place_of(delta, t, 1 - c) for delta, t in ORDER]
    for copy in loads:
        copy.wait()

    core_copies = [
        remote(ds.at[k], dr.at[k], ds_s.at[k], ds_r.at[k], sibling, s) for k in range(8)
    ]
    ds[0] = g[theirs[0]]
    pl.semaphore_wait(barrier, 2 * (REP - 1) + ZS - 1 + XS - 1)
    core_copies[0].start()
    for k in range(1, 8):
        ds[k] = g[theirs[k]]
        core_copies[k].start()

    def chip_sum(k, part):
        at = pl.ds(PART * part, PART)
        return g[mine[k], at, :].astype(F32) + dr[k, at, :].astype(F32)

    targets = (rep_at(2), rep_at(REP - 2))

    def ring(way, n):
        return remote(ys.at[way, n], yr.at[way, n], y_s.at[way, n], y_r.at[way, n], targets[way], s)

    def send(way, n, value):
        ys[way, n] = value.astype(BF16)
        ring(way, n).start()

    def got(way, n):
        ring(way, n).wait_recv()
        return yr[way, n].astype(F32)

    def far_and_near(t):
        k, n = 4 * t, 3 * t
        core_copies[k].wait_recv()
        send(0, n, chip_sum(k, 0))
        send(1, n, chip_sum(k, 1))
        core_copies[k + 1].wait_recv()
        send(0, n + 1, chip_sum(k + 1, 1))
        core_copies[k + 2].wait_recv()
        send(1, n + 1, chip_sum(k + 2, 0))

    def onward(t):
        k, n = 4 * t, 3 * t
        send(0, n + 2, chip_sum(k + 1, 0) + got(0, n))
        send(1, n + 2, chip_sum(k + 2, 1) + got(1, n))

    def arrived(t, part):
        k, n = 4 * t, 3 * t
        if part == 0:
            return chip_sum(k + 3, 0) + got(1, n + 1) + got(0, n + 2)
        return chip_sum(k + 3, 1) + got(0, n + 1) + got(1, n + 2)

    far_and_near(0)
    onward(0)
    far_and_near(1)
    core_copies[3].wait_recv()
    cross = [
        remote(xs.at[h], blk.at[rows(p * HALF + h * PART, PART)], x_s.at[h], x_r.at[h], r, pair) for h in range(2)
    ]
    for h in range(2):
        xs[h] = arrived(0, h).astype(BF16)
        cross[h].start()
    onward(1)
    core_copies[7].wait_recv()
    for h in range(2):
        blk[rows(p * HALF + h * PART, PART), :] = arrived(1, h).astype(BF16)
    for copy in late:
        copy.wait()
    for h in range(2):
        cross[h].wait_recv()

    for h in range(2):
        at = pl.ds(h * HALF, HALF)
        hp[at, :] = jnp.dot(blk[at, :], rrt[...], preferred_element_type=F32).astype(BF16)
    starts = ((1 - p) * HALF, p * HALF)
    mids = (mid0, mid1)

    def spread(q, k, away):
        base = starts[0] if away else starts[1]
        index = 8 * away + k
        return remote(
            pre.at[rows(base + q * PART + rep_at(k) * PIECE, PIECE)],
            mids[q].at[2 * r + p],
            a_s.at[q, index],
            a_r.at[q, 2 * r + p],
            rep_at(k),
            pair if away else s,
        )

    for away in (1, 0):
        at = rows(starts[1 - away], HALF)
        pre[at, :] = jnp.dot(lrt[at, :], hp[...], preferred_element_type=F32).astype(BF16)
    for q in range(2):
        for k in range(REP):
            spread(q, k, 1).start()
            if k:
                spread(q, k, 0).start()
        mids[q][2 * r + p] = pre[rows(starts[1] + q * PART + r * PIECE, PIECE), :]

    zb[z, 0:8, :] = squares(blk)
    zb[z, 8:16, :] = squares(pre)

    def tell(buf, me, send_sems, recv_sems, k, rep, shard):
        return remote(buf.at[me], buf.at[me], send_sems.at[k], recv_sems.at[me], rep, shard)

    def heard(buf, who, recv_sems):
        remote(buf.at[who], buf.at[who], recv_sems.at[who], recv_sems.at[who], r, pair).wait_recv()

    z_sends = [tell(zb, z, z_s, z_r, k, r, z_at(k)) for k in range(1, ZS)]
    for copy in z_sends:
        copy.start()

    def left_step(m, carry):
        at = rows(m * PART, PART)
        gram = lax.dot_general(blk[at, :], blk[...], (((1,), (1,)), ((), ())), preferred_element_type=F32)
        lst[at, :] = 0.95 * lst[at, :] + 0.05 * gram
        return carry

    lax.fori_loop(0, BLK // PART, left_step, 0)
    put_left = pltpu.make_async_copy(lst, new_left.at[0, 0, 0], o_s.at[0])
    put_left.start()

    for k in range(1, ZS):
        heard(zb, lax.rem(z + k, ZS), z_r)
    xb[x] = jnp.sum(zb[...], axis=0)
    x_sends = [tell(xb, x, v_s, v_r, k, r, x_at(k)) for k in range(1, XS)]
    for copy in x_sends:
        copy.start()

    def collect(q, k):
        target = rep_at(k)
        return remote(
            sb.at[q, k],
            col.at[rows(q * PART + r * PIECE, PIECE)],
            b_s.at[q, k],
            b_r.at[q, r],
            target,
            s,
        )

    def deal(q):
        for k in range(REP):
            for parity in (0, 1):
                if k == 0 and parity == 0:
                    continue
                who = 2 * rep_at(k) + (p if parity == 0 else 1 - p)
                remote(mids[q].at[who], mids[q].at[who], a_r.at[q, who], a_r.at[q, who], r, pair).wait_recv()
        for k in range(1, REP):
            target = rep_at(k)
            for n in range(2):
                sb[q, k, :, pl.ds(BLK * n, BLK)] = mids[q][tab[s // 2, 2 * target + n]]
            collect(q, k).start()
        for n in range(2):
            col[rows(q * PART + r * PIECE, PIECE), pl.ds(BLK * n, BLK)] = mids[q][tab[s // 2, 2 * r + n]]

    deal(0)
    for k in range(1, XS):
        heard(xb, lax.rem(x + k, XS), v_r)
    rb[r] = jnp.sum(xb[...], axis=0)
    r_sends = [tell(rb, r, r_s, r_r, k, rep_at(k), s) for k in range(1, REP)]
    for copy in r_sends:
        copy.start()
    deal(1)

    def right_step(m, carry):
        at = rows(m * PART, PART)
        gram = lax.dot_general(blk[:, at], blk[...], (((0,), (0,)), ((), ())), preferred_element_type=F32)
        rst[at, :] = 0.95 * rst[at, :] + 0.05 * gram
        return carry

    lax.fori_loop(0, BLK // PART, right_step, 0)
    put_right = pltpu.make_async_copy(rst, new_right.at[0, 0, 0], o_s.at[1])
    put_right.start()

    for k in range(1, REP):
        heard(rb, rep_at(k), r_r)
    totals = jnp.sum(rb[...], axis=0)
    grad_square = jnp.sum(totals[0:8, :], keepdims=True)
    pre_square = jnp.sum(totals[8:16, :], keepdims=True)
    ratio = jnp.sqrt(grad_square + 1e-06) / jnp.sqrt(pre_square + 1e-06)

    for q in range(2):
        for k in range(1, REP):
            who = rep_at(k)
            at = rows(q * PART + who * PIECE, PIECE)
            remote(col.at[at], col.at[at], b_r.at[q, who], b_r.at[q, who], r, pair).wait_recv()
        at = pl.ds(q * PART, PART)
        out[at, :] = (col[at, :].astype(F32) * ratio).astype(BF16)
        pltpu.make_async_copy(out.at[at], update.at[at], o_s.at[2 + q]).start()

    for copy in core_copies + cross + z_sends + x_sends + r_sends:
        copy.wait_send()
    for way in range(2):
        for n in range(6):
            ring(way, n).wait_send()
    for q in range(2):
        for k in range(REP):
            spread(q, k, 1).wait_send()
            if k:
                spread(q, k, 0).wait_send()
                collect(q, k).wait_send()
    put_left.wait()
    put_right.wait()
    for q in range(2):
        at = pl.ds(q * PART, PART)
        pltpu.make_async_copy(out.at[at], update.at[at], o_s.at[2 + q]).wait()


def shards(gradients, owner_table, left_stats, right_stats, left_root, right_root):
    anywhere = pl.BlockSpec(memory_space=pl.ANY)
    dma = pltpu.SemaphoreType.DMA
    operands = (gradients, owner_table, left_stats, right_stats, left_root, right_root)
    return pl.pallas_call(
        kernel,
        out_shape=(
            jax.ShapeDtypeStruct(left_stats.shape, F32),
            jax.ShapeDtypeStruct(right_stats.shape, F32),
            jax.ShapeDtypeStruct((HALF, 2 * BLK), BF16),
        ),
        in_specs=[anywhere] * 6,
        out_specs=(anywhere,) * 3,
        scratch_shapes=[
            pltpu.VMEM((16, HALF, BLK), BF16),
            pltpu.SMEM((16, 16), jnp.int32),
            pltpu.SMEM((16,), jnp.int32),
            pltpu.VMEM((8, HALF, BLK), BF16),
            pltpu.VMEM((8, HALF, BLK), BF16),
            pltpu.VMEM((2, 6, PART, BLK), BF16),
            pltpu.VMEM((2, 6, PART, BLK), BF16),
            pltpu.VMEM((2, PART, BLK), BF16),
            pltpu.VMEM((BLK, BLK), BF16),
            pltpu.VMEM((BLK, BLK), F32),
            pltpu.VMEM((BLK, BLK), F32),
            pltpu.VMEM((BLK, BLK), BF16),
            pltpu.VMEM((BLK, BLK), BF16),
            pltpu.VMEM((BLK, BLK), BF16),
            pltpu.VMEM((BLK, BLK), BF16),
            pltpu.VMEM((16, PIECE, BLK), BF16),
            pltpu.VMEM((16, PIECE, BLK), BF16),
            pltpu.VMEM((2, REP, PIECE, 2 * BLK), BF16),
            pltpu.VMEM((HALF, 2 * BLK), BF16),
            pltpu.VMEM((HALF, 2 * BLK), BF16),
            pltpu.VMEM((ZS, 16, 128), F32),
            pltpu.VMEM((XS, 16, 128), F32),
            pltpu.VMEM((REP, 16, 128), F32),
            dma((21,)),
            dma((8,)), dma((8,)),
            dma((2, 6)), dma((2, 6)),
            dma((2,)), dma((2,)),
            dma((2, 16)), dma((2, 16)),
            dma((2, REP)), dma((2, REP)),
            dma((ZS,)), dma((ZS,)),
            dma((XS,)), dma((XS,)),
            dma((REP,)), dma((REP,)),
            dma((4,)),
        ],
        compiler_params=pltpu.CompilerParams(
            collective_id=0, has_side_effects=True, vmem_limit_bytes=40 << 20
        ),
        name="shampoo",
    )(*(pltpu.with_memory_space_constraint(v, pltpu.HBM) for v in operands))


def solution(mesh):
    slots = P("rep", "shard", None, None, None)
    return jax.shard_map(
        shards,
        mesh=mesh,
        in_specs=(P("rep", "shard", None), P(), slots, slots, slots, slots),
        out_specs=(slots, slots, P("shard", "rep")),
        check_vma=False,
    )
```

```python
import jax
import jax.numpy as jnp
from jax import lax
from jax.experimental import pallas as pl
from jax.experimental.pallas import tpu as pltpu
from jax.sharding import PartitionSpec as P

MESH = pl.DeviceIdType.MESH
F32 = jnp.float32
BF16 = jnp.bfloat16
REP = 8
YS = 4
XS = 4
ZS = 8
BLK = 512
HALF = 256
PART = 128
PIECE = 16
ORDER = ((2, 0), (1, 0), (3, 0), (0, 0), (2, 1), (1, 1), (3, 1), (0, 1))


def remote(src, dst, send, recv, rep, shard):
    return pltpu.make_async_remote_copy(
        src_ref=src, dst_ref=dst, send_sem=send, recv_sem=recv, device_id=(rep, shard), device_id_type=MESH
    )


def rows(start, size):
    return pl.ds(pl.multiple_of(start, size), size)


def squares(ref):
    def step(m, total):
        value = ref[rows(m * 32, 32), :].astype(F32)
        value = value * value
        for a in range(4):
            for b in range(4):
                total = total + value[8 * a : 8 * a + 8, 128 * b : 128 * b + 128]
        return total

    return lax.fori_loop(0, BLK // 32, step, jnp.zeros((8, 128), F32))


def kernel(
    grads, table, lstat, rstat, lroot, rroot, new_left, new_right, update,
    g, tab, inv, ds, dr, ys, yr, xs, blk, lst, rst, lrt, rrt, hp, pre, mid0, mid1, sb, col, out, zb, xb, rb,
    ld, ds_s, ds_r, y_s, y_r, x_s, x_r, a_s, a_r, b_s, b_r, z_s, z_r, v_s, v_r, r_s, r_r, o_s, z_in,
):
    r = lax.axis_index("rep")
    s = lax.axis_index("shard")
    y, c = r // 2, lax.rem(r, 2)
    p = lax.rem(s, 2)
    z, x = s // XS, lax.rem(s, XS)
    pair = s + 1 - 2 * p
    sibling = r + 1 - 2 * c

    def rep_at(k):
        return lax.rem(r + k, REP)

    def x_at(k):
        return z * XS + lax.rem(x + k, XS)

    def z_at(k):
        return lax.rem(z + k, ZS) * XS + x

    barrier = pltpu.get_barrier_semaphore()

    def greet(rep, shard):
        pl.semaphore_signal(barrier, inc=1, device_id=(rep, shard), device_id_type=MESH)

    get_table = pltpu.make_async_copy(table, tab, ld.at[16])
    get_table.start()
    loads = [
        pltpu.make_async_copy(grads.at[0, :, pl.ds(BLK * j, BLK)], g.at[j], ld.at[j]) for j in range(16)
    ]
    for copy in loads:
        copy.start()
    late = [
        pltpu.make_async_copy(src.at[0, 0, 0], dst, ld.at[17 + n])
        for n, (src, dst) in enumerate(((rroot, rrt), (lroot, lrt), (lstat, lst), (rstat, rst)))
    ]

    below, above = z > 0, z < ZS - 1
    greet(sibling, s)
    for rep, shard in ((rep_at(2), s), (rep_at(REP - 2), s), (r, x_at(1)), (r, x_at(XS - 1))):
        greet(rep, shard)
    pl.when(below)(lambda: greet(r, s - XS))
    pl.when(above)(lambda: greet(r, s + XS))

    get_table.wait()
    owners = [tab[s // 2, j] for j in range(16)]

    def invert(v, carry):
        place = jnp.int32(0)
        for j in range(1, 16):
            place = jnp.where(owners[j] == v, j, place)
        inv[v] = place
        return carry

    lax.fori_loop(0, 16, invert, 0)

    def place_of(delta, t, core):
        return inv[4 * lax.rem(y + delta, YS) + 2 * core + (p if t else 1 - p)]

    mine = [place_of(delta, t, c) for delta, t in ORDER]
    theirs = [place_of(delta, t, 1 - c) for delta, t in ORDER]
    for copy in loads:
        copy.wait()
    for copy in late:
        copy.start()

    core_copies = [
        remote(ds.at[k], dr.at[k], ds_s.at[k], ds_r.at[k], sibling, s) for k in range(8)
    ]
    ds[0] = g[theirs[0]]
    pl.semaphore_wait(barrier, 5 + below.astype(jnp.int32) + above.astype(jnp.int32))
    core_copies[0].start()
    for k in range(1, 8):
        ds[k] = g[theirs[k]]
        core_copies[k].start()

    def pass_on(n):
        far = (1 << n) * XS

        def note(shard):
            pl.semaphore_signal(z_in.at[n], inc=1, device_id=(r, shard), device_id_type=MESH)

        pl.when(z >= (1 << n))(lambda: note(s - far))
        pl.when(z < ZS - (1 << n))(lambda: note(s + far))

    def passed_on(n):
        count = (z >= (1 << n)).astype(jnp.int32) + (z < ZS - (1 << n)).astype(jnp.int32)
        pl.semaphore_wait(z_in.at[n], count)

    pass_on(0)

    def chip_sum(k, part):
        at = pl.ds(PART * part, PART)
        return g[mine[k], at, :].astype(F32) + dr[k, at, :].astype(F32)

    targets = (rep_at(2), rep_at(REP - 2))

    def ring(way, n):
        return remote(ys.at[way, n], yr.at[way, n], y_s.at[way, n], y_r.at[way, n], targets[way], s)

    def send(way, n, value):
        ys[way, n] = value.astype(BF16)
        ring(way, n).start()

    def got(way, n):
        ring(way, n).wait_recv()
        return yr[way, n].astype(F32)

    def far_and_near(t):
        k, n = 4 * t, 3 * t
        core_copies[k].wait_recv()
        send(0, n, chip_sum(k, 0))
        send(1, n, chip_sum(k, 1))
        core_copies[k + 1].wait_recv()
        send(0, n + 1, chip_sum(k + 1, 1))
        core_copies[k + 2].wait_recv()
        send(1, n + 1, chip_sum(k + 2, 0))

    def onward(t):
        k, n = 4 * t, 3 * t
        send(0, n + 2, chip_sum(k + 1, 0) + got(0, n))
        send(1, n + 2, chip_sum(k + 2, 1) + got(1, n))

    def arrived(t, part):
        k, n = 4 * t, 3 * t
        if part == 0:
            return chip_sum(k + 3, 0) + got(1, n + 1) + got(0, n + 2)
        return chip_sum(k + 3, 1) + got(0, n + 1) + got(1, n + 2)

    far_and_near(0)
    onward(0)
    far_and_near(1)
    passed_on(0)
    pass_on(1)
    core_copies[3].wait_recv()
    cross = [
        remote(xs.at[h], blk.at[rows(p * HALF + h * PART, PART)], x_s.at[h], x_r.at[h], r, pair) for h in range(2)
    ]
    for h in range(2):
        xs[h] = arrived(0, h).astype(BF16)
        cross[h].start()
    onward(1)
    passed_on(1)
    pass_on(2)
    core_copies[7].wait_recv()
    for h in range(2):
        blk[rows(p * HALF + h * PART, PART), :] = arrived(1, h).astype(BF16)
    for copy in late:
        copy.wait()
    for h in range(2):
        cross[h].wait_recv()

    for h in range(2):
        at = pl.ds(h * HALF, HALF)
        hp[at, :] = jnp.dot(blk[at, :], rrt[...], preferred_element_type=F32).astype(BF16)
    starts = ((1 - p) * HALF, p * HALF)
    mids = (mid0, mid1)

    def spread(q, k, away):
        base = starts[0] if away else starts[1]
        index = 8 * away + k
        return remote(
            pre.at[rows(base + q * PART + rep_at(k) * PIECE, PIECE)],
            mids[q].at[2 * r + p],
            a_s.at[q, index],
            a_r.at[q, 2 * r + p],
            rep_at(k),
            pair if away else s,
        )

    for away in (1, 0):
        at = rows(starts[1 - away], HALF)
        pre[at, :] = jnp.dot(lrt[at, :], hp[...], preferred_element_type=F32).astype(BF16)
    def spread_all(q):
        for k in range(REP):
            spread(q, k, 1).start()
            if k:
                spread(q, k, 0).start()
        mids[q][2 * r + p] = pre[rows(starts[1] + q * PART + r * PIECE, PIECE), :]

    def tell(buf, me, send_sems, recv_sems, k, rep, shard):
        return remote(buf.at[me], buf.at[me], send_sems.at[k], recv_sems.at[me], rep, shard)

    def heard(buf, who, recv_sems):
        remote(buf.at[who], buf.at[who], recv_sems.at[who], recv_sems.at[who], r, pair).wait_recv()

    r_sends = [tell(rb, r, r_s, r_r, k, rep_at(k), s) for k in range(1, REP)]
    x_sends = [tell(xb, x, v_s, v_r, k, r, x_at(k)) for k in range(1, XS)]
    z_sends = [tell(zb, z, z_s, z_r, k, r, z_at(k)) for k in range(1, ZS)]

    spread_all(0)
    zb[z, 0:8, :] = squares(blk)
    zb[z, 8:16, :] = squares(pre)
    passed_on(2)
    for copy in z_sends:
        copy.start()
    spread_all(1)

    def left_step(m, carry):
        at = rows(m * PART, PART)
        gram = lax.dot_general(blk[at, :], blk[...], (((1,), (1,)), ((), ())), preferred_element_type=F32)
        lst[at, :] = 0.95 * lst[at, :] + 0.05 * gram
        return carry

    lax.fori_loop(0, BLK // PART, left_step, 0)
    put_left = pltpu.make_async_copy(lst, new_left.at[0, 0, 0], o_s.at[0])
    put_left.start()

    def collect(q, k):
        target = rep_at(k)
        return remote(
            sb.at[q, k],
            col.at[rows(q * PART + r * PIECE, PIECE)],
            b_s.at[q, k],
            b_r.at[q, r],
            target,
            s,
        )

    def deal(q):
        for k in range(REP):
            for parity in (0, 1):
                if k == 0 and parity == 0:
                    continue
                who = 2 * rep_at(k) + (p if parity == 0 else 1 - p)
                remote(mids[q].at[who], mids[q].at[who], a_r.at[q, who], a_r.at[q, who], r, pair).wait_recv()
        for k in range(1, REP):
            target = rep_at(k)
            for n in range(2):
                sb[q, k, :, pl.ds(BLK * n, BLK)] = mids[q][tab[s // 2, 2 * target + n]]
            collect(q, k).start()
        for n in range(2):
            col[rows(q * PART + r * PIECE, PIECE), pl.ds(BLK * n, BLK)] = mids[q][tab[s // 2, 2 * r + n]]

    deal(0)
    for k in range(1, ZS):
        heard(zb, lax.rem(z + k, ZS), z_r)
    xb[x] = jnp.sum(zb[...], axis=0)
    for copy in x_sends:
        copy.start()

    deal(1)
    for k in range(1, XS):
        heard(xb, lax.rem(x + k, XS), v_r)
    rb[r] = jnp.sum(xb[...], axis=0)
    for copy in r_sends:
        copy.start()
    def right_step(m, carry):
        at = rows(m * PART, PART)
        gram = lax.dot_general(blk[:, at], blk[...], (((0,), (0,)), ((), ())), preferred_element_type=F32)
        rst[at, :] = 0.95 * rst[at, :] + 0.05 * gram
        return carry

    lax.fori_loop(0, BLK // PART, right_step, 0)
    put_right = pltpu.make_async_copy(rst, new_right.at[0, 0, 0], o_s.at[1])
    put_right.start()

    for k in range(1, REP):
        heard(rb, rep_at(k), r_r)
    totals = jnp.sum(rb[...], axis=0)
    grad_square = jnp.sum(totals[0:8, :], keepdims=True)
    pre_square = jnp.sum(totals[8:16, :], keepdims=True)
    ratio = jnp.sqrt(grad_square + 1e-06) / jnp.sqrt(pre_square + 1e-06)

    for q in range(2):
        for k in range(1, REP):
            who = rep_at(k)
            at = rows(q * PART + who * PIECE, PIECE)
            remote(col.at[at], col.at[at], b_r.at[q, who], b_r.at[q, who], r, pair).wait_recv()
        at = pl.ds(q * PART, PART)
        out[at, :] = (col[at, :].astype(F32) * ratio).astype(BF16)
        pltpu.make_async_copy(out.at[at], update.at[at], o_s.at[2 + q]).start()

    for copy in core_copies + cross + z_sends + x_sends + r_sends:
        copy.wait_send()
    for way in range(2):
        for n in range(6):
            ring(way, n).wait_send()
    for q in range(2):
        for k in range(REP):
            spread(q, k, 1).wait_send()
            if k:
                spread(q, k, 0).wait_send()
                collect(q, k).wait_send()
    put_left.wait()
    put_right.wait()
    for q in range(2):
        at = pl.ds(q * PART, PART)
        pltpu.make_async_copy(out.at[at], update.at[at], o_s.at[2 + q]).wait()


def put_out(a, b, c, out_a, out_b, out_c, sems):
    copies = [
        pltpu.make_async_copy(src, dst, sems.at[n]) for n, (src, dst) in enumerate(((c, out_c), (a, out_a), (b, out_b)))
    ]
    for copy in copies:
        copy.start()
    for copy in copies:
        copy.wait()


def shards(gradients, owner_table, left_stats, right_stats, left_root, right_root):
    anywhere = pl.BlockSpec(memory_space=pl.ANY)
    dma = pltpu.SemaphoreType.DMA
    operands = (gradients, owner_table, left_stats, right_stats, left_root, right_root)
    results = pl.pallas_call(
        kernel,
        out_shape=(
            pltpu.VMEM(left_stats.shape, F32),
            pltpu.VMEM(right_stats.shape, F32),
            pltpu.VMEM((HALF, 2 * BLK), BF16),
        ),
        in_specs=[anywhere] * 6,
        out_specs=(anywhere,) * 3,
        scratch_shapes=[
            pltpu.VMEM((16, HALF, BLK), BF16),
            pltpu.SMEM((16, 16), jnp.int32),
            pltpu.SMEM((16,), jnp.int32),
            pltpu.VMEM((8, HALF, BLK), BF16),
            pltpu.VMEM((8, HALF, BLK), BF16),
            pltpu.VMEM((2, 6, PART, BLK), BF16),
            pltpu.VMEM((2, 6, PART, BLK), BF16),
            pltpu.VMEM((2, PART, BLK), BF16),
            pltpu.VMEM((BLK, BLK), BF16),
            pltpu.VMEM((BLK, BLK), F32),
            pltpu.VMEM((BLK, BLK), F32),
            pltpu.VMEM((BLK, BLK), BF16),
            pltpu.VMEM((BLK, BLK), BF16),
            pltpu.VMEM((BLK, BLK), BF16),
            pltpu.VMEM((BLK, BLK), BF16),
            pltpu.VMEM((16, PIECE, BLK), BF16),
            pltpu.VMEM((16, PIECE, BLK), BF16),
            pltpu.VMEM((2, REP, PIECE, 2 * BLK), BF16),
            pltpu.VMEM((HALF, 2 * BLK), BF16),
            pltpu.VMEM((HALF, 2 * BLK), BF16),
            pltpu.VMEM((ZS, 16, 128), F32),
            pltpu.VMEM((XS, 16, 128), F32),
            pltpu.VMEM((REP, 16, 128), F32),
            dma((21,)),
            dma((8,)), dma((8,)),
            dma((2, 6)), dma((2, 6)),
            dma((2,)), dma((2,)),
            dma((2, 16)), dma((2, 16)),
            dma((2, REP)), dma((2, REP)),
            dma((ZS,)), dma((ZS,)),
            dma((XS,)), dma((XS,)),
            dma((REP,)), dma((REP,)),
            dma((4,)),
            pltpu.SemaphoreType.REGULAR((3,)),
        ],
        compiler_params=pltpu.CompilerParams(
            collective_id=0, has_side_effects=True, vmem_limit_bytes=40 << 20
        ),
        name="shampoo",
    )(*(pltpu.with_memory_space_constraint(v, pltpu.HBM) for v in operands))
    return pl.pallas_call(
        put_out,
        out_shape=tuple(jax.ShapeDtypeStruct(v.shape, v.dtype) for v in results),
        in_specs=[anywhere] * 3,
        out_specs=(anywhere,) * 3,
        scratch_shapes=[dma((3,))],
        compiler_params=pltpu.CompilerParams(vmem_limit_bytes=4 << 20),
        name="put_out",
    )(*(pltpu.with_memory_space_constraint(v, pltpu.VMEM) for v in results))


def solution(mesh):
    slots = P("rep", "shard", None, None, None)
    return jax.shard_map(
        shards,
        mesh=mesh,
        in_specs=(P("rep", "shard", None), P(), slots, slots, slots, slots),
        out_specs=(slots, slots, P("shard", "rep")),
        check_vma=False,
    )
```

```python
import jax
import jax.numpy as jnp
from jax import lax
from jax.experimental import pallas as pl
from jax.experimental.pallas import tpu as pltpu
from jax.sharding import PartitionSpec as P

MESH = pl.DeviceIdType.MESH
F32 = jnp.float32
BF16 = jnp.bfloat16
REP = 8
YS = 4
XS = 4
ZS = 8
BLK = 512
HALF = 256
PART = 128
PIECE = 16
ORDER = ((2, 0), (1, 0), (3, 0), (0, 0), (2, 1), (1, 1), (3, 1), (0, 1))


def remote(src, dst, send, recv, rep, shard):
    return pltpu.make_async_remote_copy(
        src_ref=src, dst_ref=dst, send_sem=send, recv_sem=recv, device_id=(rep, shard), device_id_type=MESH
    )


def rows(start, size):
    return pl.ds(pl.multiple_of(start, size), size)


def squares(ref):
    def step(m, total):
        value = ref[rows(m * 32, 32), :].astype(F32)
        value = value * value
        for a in range(4):
            for b in range(4):
                total = total + value[8 * a : 8 * a + 8, 128 * b : 128 * b + 128]
        return total

    return lax.fori_loop(0, BLK // 32, step, jnp.zeros((8, 128), F32))


def kernel(
    grads, table, lstat, rstat, lroot, rroot, new_left, new_right, update,
    g, tab, inv, ds, dr, ys, yr, xs, blk, lst, rst, lrt, rrt, hp, pre, mid0, mid1, sb, col, out, zb, xb, rb,
    ld, ds_s, ds_r, y_s, y_r, x_s, x_r, a_s, a_r, b_s, b_r, z_q, x_q, r_q, o_s, z_in,
):
    r = lax.axis_index("rep")
    s = lax.axis_index("shard")
    y, c = r // 2, lax.rem(r, 2)
    p = lax.rem(s, 2)
    z, x = s // XS, lax.rem(s, XS)
    pair = s + 1 - 2 * p
    sibling = r + 1 - 2 * c

    def rep_at(k):
        return lax.rem(r + k, REP)

    def x_at(k):
        return z * XS + lax.rem(x + k, XS)

    def z_at(k):
        return lax.rem(z + k, ZS) * XS + x

    barrier = pltpu.get_barrier_semaphore()

    def greet(rep, shard):
        pl.semaphore_signal(barrier, inc=1, device_id=(rep, shard), device_id_type=MESH)

    get_table = pltpu.make_async_copy(table, tab, ld.at[1])
    get_table.start()
    loads = [
        pltpu.make_async_copy(grads.at[0, :, pl.ds(BLK * j, BLK)], g.at[j], ld.at[0]) for j in range(16)
    ]
    for copy in loads:
        copy.start()
    late = [
        pltpu.make_async_copy(src.at[0, 0, 0], dst, ld.at[2 + n])
        for n, (src, dst) in enumerate(((rroot, rrt), (lroot, lrt), (lstat, lst), (rstat, rst)))
    ]

    below, above = z > 0, z < ZS - 1
    greet(sibling, s)
    for rep, shard in ((rep_at(2), s), (rep_at(REP - 2), s), (r, x_at(1)), (r, x_at(XS - 1))):
        greet(rep, shard)
    pl.when(below)(lambda: greet(r, s - XS))
    pl.when(above)(lambda: greet(r, s + XS))

    get_table.wait()
    owners = [tab[s // 2, j] for j in range(16)]

    def invert(v, carry):
        place = jnp.int32(0)
        for j in range(1, 16):
            place = jnp.where(owners[j] == v, j, place)
        inv[v] = place
        return carry

    lax.fori_loop(0, 16, invert, 0)

    def place_of(delta, t, core):
        return inv[4 * lax.rem(y + delta, YS) + 2 * core + (p if t else 1 - p)]

    mine = [place_of(delta, t, c) for delta, t in ORDER]
    theirs = [place_of(delta, t, 1 - c) for delta, t in ORDER]
    pltpu.make_async_copy(g, g, ld.at[0]).wait()
    for copy in late:
        copy.start()

    core_copies = [
        remote(ds.at[k], dr.at[k], ds_s.at[0], ds_r.at[k], sibling, s) for k in range(8)
    ]
    ds[0] = g[theirs[0]]
    pl.semaphore_wait(barrier, 5 + below.astype(jnp.int32) + above.astype(jnp.int32))
    core_copies[0].start()
    for k in range(1, 8):
        ds[k] = g[theirs[k]]
        core_copies[k].start()

    def pass_on(n):
        far = (1 << n) * XS

        def note(shard):
            pl.semaphore_signal(z_in.at[n], inc=1, device_id=(r, shard), device_id_type=MESH)

        pl.when(z >= (1 << n))(lambda: note(s - far))
        pl.when(z < ZS - (1 << n))(lambda: note(s + far))

    def passed_on(n):
        count = (z >= (1 << n)).astype(jnp.int32) + (z < ZS - (1 << n)).astype(jnp.int32)
        pl.semaphore_wait(z_in.at[n], count)

    pass_on(0)

    def chip_sum(k, part):
        at = pl.ds(PART * part, PART)
        return g[mine[k], at, :].astype(F32) + dr[k, at, :].astype(F32)

    targets = (rep_at(2), rep_at(REP - 2))

    def ring(way, n):
        return remote(ys.at[way, n], yr.at[way, n], y_s.at[0], y_r.at[way, n], targets[way], s)

    def send(way, n, value):
        ys[way, n] = value.astype(BF16)
        ring(way, n).start()

    def got(way, n):
        ring(way, n).wait_recv()
        return yr[way, n].astype(F32)

    def far_and_near(t):
        k, n = 4 * t, 3 * t
        core_copies[k].wait_recv()
        send(0, n, chip_sum(k, 0))
        send(1, n, chip_sum(k, 1))
        core_copies[k + 1].wait_recv()
        send(0, n + 1, chip_sum(k + 1, 1))
        core_copies[k + 2].wait_recv()
        send(1, n + 1, chip_sum(k + 2, 0))

    def onward(t):
        k, n = 4 * t, 3 * t
        send(0, n + 2, chip_sum(k + 1, 0) + got(0, n))
        send(1, n + 2, chip_sum(k + 2, 1) + got(1, n))

    def arrived(t, part):
        k, n = 4 * t, 3 * t
        if part == 0:
            return chip_sum(k + 3, 0) + got(1, n + 1) + got(0, n + 2)
        return chip_sum(k + 3, 1) + got(0, n + 1) + got(1, n + 2)

    far_and_near(0)
    onward(0)
    far_and_near(1)
    passed_on(0)
    pass_on(1)
    core_copies[3].wait_recv()
    cross = [
        remote(xs.at[h], blk.at[rows(p * HALF + h * PART, PART)], x_s.at[0], x_r.at[h], r, pair) for h in range(2)
    ]
    for h in range(2):
        xs[h] = arrived(0, h).astype(BF16)
        cross[h].start()
    onward(1)
    passed_on(1)
    pass_on(2)
    core_copies[7].wait_recv()
    for h in range(2):
        blk[rows(p * HALF + h * PART, PART), :] = arrived(1, h).astype(BF16)
    for copy in late:
        copy.wait()
    for h in range(2):
        cross[h].wait_recv()

    for h in range(2):
        at = pl.ds(h * HALF, HALF)
        hp[at, :] = jnp.dot(blk[at, :], rrt[...], preferred_element_type=F32).astype(BF16)
    starts = ((1 - p) * HALF, p * HALF)
    mids = (mid0, mid1)

    def spread(q, k, away):
        base = starts[0] if away else starts[1]
        return remote(
            pre.at[rows(base + q * PART + rep_at(k) * PIECE, PIECE)],
            mids[q].at[2 * r + p],
            a_s.at[q],
            a_r.at[q],
            rep_at(k),
            pair if away else s,
        )

    for away in (1, 0):
        at = rows(starts[1 - away], HALF)
        pre[at, :] = jnp.dot(lrt[at, :], hp[...], preferred_element_type=F32).astype(BF16)
    def spread_done(q):
        pieces = mids[q].at[pl.ds(0, 15)]
        return remote(pieces, pieces, a_s.at[q], a_r.at[q], r, pair)

    def spread_all(q):
        for k in range(REP):
            spread(q, k, 1).start()
            if k:
                spread(q, k, 0).start()
        mids[q][2 * r + p] = pre[rows(starts[1] + q * PART + r * PIECE, PIECE), :]

    def tell(buf, me, sems, rep, shard):
        return remote(buf.at[me], buf.at[me], sems.at[0], sems.at[1], rep, shard)

    def told(buf, count, sems):
        others = buf.at[pl.ds(0, count - 1)]
        return remote(others, others, sems.at[0], sems.at[1], r, pair)

    z_sends = [tell(zb, z, z_q, r, z_at(k)) for k in range(1, ZS)]
    x_sends = [tell(xb, x, x_q, r, x_at(k)) for k in range(1, XS)]
    r_sends = [tell(rb, r, r_q, rep_at(k), s) for k in range(1, REP)]

    spread_all(0)
    zb[z, 0:8, :] = squares(blk)
    zb[z, 8:16, :] = squares(pre)
    passed_on(2)
    for copy in z_sends:
        copy.start()
    spread_all(1)

    def left_step(m, carry):
        at = rows(m * PART, PART)
        gram = lax.dot_general(blk[at, :], blk[...], (((1,), (1,)), ((), ())), preferred_element_type=F32)
        lst[at, :] = 0.95 * lst[at, :] + 0.05 * gram
        return carry

    lax.fori_loop(0, BLK // PART, left_step, 0)
    put_left = pltpu.make_async_copy(lst, new_left.at[0, 0, 0], o_s.at[0])
    put_left.start()

    def collect(q, k):
        target = rep_at(k)
        return remote(
            sb.at[q, k],
            col.at[rows(q * PART + r * PIECE, PIECE)],
            b_s.at[q],
            b_r.at[q],
            target,
            s,
        )

    def collect_done(q):
        pieces = sb.at[q, pl.ds(1, REP - 1)]
        return remote(pieces, pieces, b_s.at[q], b_r.at[q], r, pair)

    def deal(q):
        spread_done(q).wait_recv()
        for k in range(1, REP):
            target = rep_at(k)
            for n in range(2):
                sb[q, k, :, pl.ds(BLK * n, BLK)] = mids[q][tab[s // 2, 2 * target + n]]
            collect(q, k).start()
        for n in range(2):
            col[rows(q * PART + r * PIECE, PIECE), pl.ds(BLK * n, BLK)] = mids[q][tab[s // 2, 2 * r + n]]

    deal(0)
    told(zb, ZS, z_q).wait_recv()
    xb[x] = jnp.sum(zb[...], axis=0)
    for copy in x_sends:
        copy.start()

    deal(1)
    told(xb, XS, x_q).wait_recv()
    rb[r] = jnp.sum(xb[...], axis=0)
    for copy in r_sends:
        copy.start()
    def right_step(m, carry):
        at = rows(m * PART, PART)
        gram = lax.dot_general(blk[:, at], blk[...], (((0,), (0,)), ((), ())), preferred_element_type=F32)
        rst[at, :] = 0.95 * rst[at, :] + 0.05 * gram
        return carry

    lax.fori_loop(0, BLK // PART, right_step, 0)
    put_right = pltpu.make_async_copy(rst, new_right.at[0, 0, 0], o_s.at[1])
    put_right.start()


    remote(ds, dr, ds_s.at[0], ds_r.at[0], sibling, s).wait_send()
    remote(ys, yr, y_s.at[0], y_r.at[0, 0], sibling, s).wait_send()
    remote(xs, xs, x_s.at[0], x_r.at[0], r, pair).wait_send()
    told(zb, ZS, z_q).wait_send()
    told(xb, XS, x_q).wait_send()
    for q in range(2):
        spread_done(q).wait_send()

    told(rb, REP, r_q).wait_recv()
    totals = jnp.sum(rb[...], axis=0)
    grad_square = jnp.sum(totals[0:8, :], keepdims=True)
    pre_square = jnp.sum(totals[8:16, :], keepdims=True)
    ratio = jnp.sqrt(grad_square + 1e-06) / jnp.sqrt(pre_square + 1e-06)

    for q in range(2):
        collect_done(q).wait_recv()
        at = pl.ds(q * PART, PART)
        out[at, :] = (col[at, :].astype(F32) * ratio).astype(BF16)
        pltpu.make_async_copy(out.at[at], update.at[at], o_s.at[2 + q]).start()

    told(rb, REP, r_q).wait_send()
    for q in range(2):
        collect_done(q).wait_send()
    put_left.wait()
    put_right.wait()
    for q in range(2):
        at = pl.ds(q * PART, PART)
        pltpu.make_async_copy(out.at[at], update.at[at], o_s.at[2 + q]).wait()


def put_out(a, b, c, out_a, out_b, out_c, sems):
    copies = [
        pltpu.make_async_copy(src, dst, sems.at[n]) for n, (src, dst) in enumerate(((c, out_c), (a, out_a), (b, out_b)))
    ]
    for copy in copies:
        copy.start()
    for copy in copies:
        copy.wait()


def shards(gradients, owner_table, left_stats, right_stats, left_root, right_root):
    anywhere = pl.BlockSpec(memory_space=pl.ANY)
    dma = pltpu.SemaphoreType.DMA
    operands = (gradients, owner_table, left_stats, right_stats, left_root, right_root)
    results = pl.pallas_call(
        kernel,
        out_shape=(
            pltpu.VMEM(left_stats.shape, F32),
            pltpu.VMEM(right_stats.shape, F32),
            pltpu.VMEM((HALF, 2 * BLK), BF16),
        ),
        in_specs=[anywhere] * 6,
        out_specs=(anywhere,) * 3,
        scratch_shapes=[
            pltpu.VMEM((16, HALF, BLK), BF16),
            pltpu.SMEM((16, 16), jnp.int32),
            pltpu.SMEM((16,), jnp.int32),
            pltpu.VMEM((8, HALF, BLK), BF16),
            pltpu.VMEM((8, HALF, BLK), BF16),
            pltpu.VMEM((2, 6, PART, BLK), BF16),
            pltpu.VMEM((2, 6, PART, BLK), BF16),
            pltpu.VMEM((2, PART, BLK), BF16),
            pltpu.VMEM((BLK, BLK), BF16),
            pltpu.VMEM((BLK, BLK), F32),
            pltpu.VMEM((BLK, BLK), F32),
            pltpu.VMEM((BLK, BLK), BF16),
            pltpu.VMEM((BLK, BLK), BF16),
            pltpu.VMEM((BLK, BLK), BF16),
            pltpu.VMEM((BLK, BLK), BF16),
            pltpu.VMEM((16, PIECE, BLK), BF16),
            pltpu.VMEM((16, PIECE, BLK), BF16),
            pltpu.VMEM((2, REP, PIECE, 2 * BLK), BF16),
            pltpu.VMEM((HALF, 2 * BLK), BF16),
            pltpu.VMEM((HALF, 2 * BLK), BF16),
            pltpu.VMEM((ZS, 16, 128), F32),
            pltpu.VMEM((XS, 16, 128), F32),
            pltpu.VMEM((REP, 16, 128), F32),
            dma((6,)),
            dma((1,)), dma((8,)),
            dma((1,)), dma((2, 6)),
            dma((1,)), dma((2,)),
            dma((2,)), dma((2,)),
            dma((2,)), dma((2,)),
            dma((2,)), dma((2,)), dma((2,)),
            dma((4,)),
            pltpu.SemaphoreType.REGULAR((3,)),
        ],
        compiler_params=pltpu.CompilerParams(
            collective_id=0, has_side_effects=True, vmem_limit_bytes=40 << 20
        ),
        name="shampoo",
    )(*(pltpu.with_memory_space_constraint(v, pltpu.HBM) for v in operands))
    return pl.pallas_call(
        put_out,
        out_shape=tuple(jax.ShapeDtypeStruct(v.shape, v.dtype) for v in results),
        in_specs=[anywhere] * 3,
        out_specs=(anywhere,) * 3,
        scratch_shapes=[dma((3,))],
        compiler_params=pltpu.CompilerParams(vmem_limit_bytes=4 << 20),
        name="put_out",
    )(*(pltpu.with_memory_space_constraint(v, pltpu.VMEM) for v in results))


def solution(mesh):
    slots = P("rep", "shard", None, None, None)
    return jax.shard_map(
        shards,
        mesh=mesh,
        in_specs=(P("rep", "shard", None), P(), slots, slots, slots, slots),
        out_specs=(slots, slots, P("shard", "rep")),
        check_vma=False,
    )
```

```python
import jax
import jax.numpy as jnp
from jax import lax
from jax.experimental import pallas as pl
from jax.experimental.pallas import tpu as pltpu
from jax.sharding import PartitionSpec as P

MESH = pl.DeviceIdType.MESH
F32 = jnp.float32
BF16 = jnp.bfloat16
REP = 8
YS = 4
XS = 4
ZS = 8
BLK = 512
HALF = 256
PART = 128
PIECE = 16
ORDER = ((2, 0), (1, 0), (3, 0), (0, 0), (2, 1), (1, 1), (3, 1), (0, 1))


def remote(src, dst, send, recv, rep, shard):
    return pltpu.make_async_remote_copy(
        src_ref=src, dst_ref=dst, send_sem=send, recv_sem=recv, device_id=(rep, shard), device_id_type=MESH
    )


def rows(start, size):
    return pl.ds(pl.multiple_of(start, size), size)


def squares(value):
    value = value.astype(F32)
    value = value * value
    parts = [value[8 * m : 8 * m + 8, 128 * n : 128 * n + 128] for m in range(value.shape[0] // 8) for n in range(4)]
    while len(parts) > 1:
        parts = [parts[m] + parts[m + 1] for m in range(0, len(parts), 2)]
    return parts[0]


def kernel(
    grads, table, lstat, rstat, lroot, rroot, new_left, new_right, update,
    top, low, tab, inv, ds, dr, ys, yr, xs, blk, lst, rst, lrt, rrt, hp, pre, mid0, mid1, sb, col, out, zb, xb, rb,
    ld, ds_s, ds_r, y_s, y_r, x_s, x_r, a_s, a_r, b_s, b_r, z_q, x_q, r_q, o_s, z_in,
):
    r = lax.axis_index("rep")
    s = lax.axis_index("shard")
    y, c = r // 2, lax.rem(r, 2)
    p = lax.rem(s, 2)
    z, x = s // XS, lax.rem(s, XS)
    pair = s + 1 - 2 * p
    sibling = r + 1 - 2 * c

    def rep_at(k):
        return lax.rem(r + k, REP)

    def x_at(k):
        return z * XS + lax.rem(x + k, XS)

    def z_at(k):
        return lax.rem(z + k, ZS) * XS + x

    barrier = pltpu.get_barrier_semaphore()

    def greet(rep, shard):
        pl.semaphore_signal(barrier, inc=1, device_id=(rep, shard), device_id_type=MESH)

    get_table = pltpu.make_async_copy(table, tab, ld.at[1])
    get_table.start()
    g = (top, low)
    loads = [
        pltpu.make_async_copy(
            grads.at[0, pl.ds(PART * part, PART), pl.ds(BLK * j, BLK)], g[part].at[j], ld.at[6 * part]
        )
        for part in range(2) for j in range(16)
    ]
    for copy in loads:
        copy.start()
    late = [
        pltpu.make_async_copy(src.at[0, 0, 0], dst, ld.at[2 + n])
        for n, (src, dst) in enumerate(((rroot, rrt), (lroot, lrt), (lstat, lst), (rstat, rst)))
    ]

    below, above = z > 0, z < ZS - 1
    greet(sibling, s)
    for rep, shard in ((rep_at(2), s), (rep_at(REP - 2), s), (r, x_at(1)), (r, x_at(XS - 1))):
        greet(rep, shard)
    pl.when(below)(lambda: greet(r, s - XS))
    pl.when(above)(lambda: greet(r, s + XS))

    get_table.wait()
    owners = [tab[s // 2, j] for j in range(16)]

    def invert(v, carry):
        place = jnp.int32(0)
        for j in range(1, 16):
            place = jnp.where(owners[j] == v, j, place)
        inv[v] = place
        return carry

    lax.fori_loop(0, 16, invert, 0)

    def place_of(delta, t, core):
        return inv[4 * lax.rem(y + delta, YS) + 2 * core + (p if t else 1 - p)]

    mine = [place_of(delta, t, c) for delta, t in ORDER]
    theirs = [place_of(delta, t, 1 - c) for delta, t in ORDER]

    def core_copy(k, part=None):
        at = pl.ds(PART * (part or 0), HALF if part is None else PART)
        return remote(ds.at[k, at], dr.at[k, at], ds_s.at[0], ds_r.at[8 if part == 1 else k], sibling, s)

    core_copies = [core_copy(k) for k in range(8)]
    firsts = [core_copy(0, part) for part in range(2)]
    for part in range(2):
        pltpu.make_async_copy(g[part], g[part], ld.at[6 * part]).wait()
        if part:
            for copy in late:
                copy.start()
        ds[0, pl.ds(PART * part, PART), :] = g[part][theirs[0]]
        if part == 0:
            pl.semaphore_wait(barrier, 5 + below.astype(jnp.int32) + above.astype(jnp.int32))
        firsts[part].start()
    for k in range(1, 8):
        for part in range(2):
            ds[k, pl.ds(PART * part, PART), :] = g[part][theirs[k]]
        core_copies[k].start()

    def pass_on(n):
        far = (1 << n) * XS

        def note(shard):
            pl.semaphore_signal(z_in.at[n], inc=1, device_id=(r, shard), device_id_type=MESH)

        pl.when(z >= (1 << n))(lambda: note(s - far))
        pl.when(z < ZS - (1 << n))(lambda: note(s + far))

    def passed_on(n):
        count = (z >= (1 << n)).astype(jnp.int32) + (z < ZS - (1 << n)).astype(jnp.int32)
        pl.semaphore_wait(z_in.at[n], count)

    pass_on(0)

    def chip_sum(k, part):
        at = pl.ds(PART * part, PART)
        return g[part][mine[k]].astype(F32) + dr[k, at, :].astype(F32)

    targets = (rep_at(2), rep_at(REP - 2))

    def ring(way, n):
        return remote(ys.at[way, n], yr.at[way, n], y_s.at[0], y_r.at[way, n], targets[way], s)

    def send(way, n, value):
        ys[way, n] = value.astype(BF16)
        ring(way, n).start()

    def got(way, n):
        ring(way, n).wait_recv()
        return yr[way, n].astype(F32)

    def far_and_near(t):
        k, n = 4 * t, 3 * t
        for way in range(2):
            if t == 0:
                firsts[way].wait_recv()
            elif way == 0:
                core_copies[k].wait_recv()
            send(way, n, chip_sum(k, way))
        core_copies[k + 1].wait_recv()
        send(0, n + 1, chip_sum(k + 1, 1))
        core_copies[k + 2].wait_recv()
        send(1, n + 1, chip_sum(k + 2, 0))

    def onward(t):
        k, n = 4 * t, 3 * t
        send(0, n + 2, chip_sum(k + 1, 0) + got(0, n))
        send(1, n + 2, chip_sum(k + 2, 1) + got(1, n))

    def arrived(t, part):
        k, n = 4 * t, 3 * t
        if part == 0:
            return chip_sum(k + 3, 0) + got(1, n + 1) + got(0, n + 2)
        return chip_sum(k + 3, 1) + got(0, n + 1) + got(1, n + 2)

    far_and_near(0)
    onward(0)
    far_and_near(1)
    passed_on(0)
    pass_on(1)
    core_copies[3].wait_recv()
    cross = [
        remote(xs.at[h], blk.at[rows(p * HALF + h * PART, PART)], x_s.at[0], x_r.at[h], r, pair) for h in range(2)
    ]
    for h in range(2):
        xs[h] = arrived(0, h).astype(BF16)
        cross[h].start()
    onward(1)
    passed_on(1)
    pass_on(2)
    core_copies[7].wait_recv()
    for h in range(2):
        blk[rows(p * HALF + h * PART, PART), :] = arrived(1, h).astype(BF16)
    for copy in late:
        copy.wait()
    for h in range(2):
        cross[h].wait_recv()

    passed_on(2)
    grad_part = pre_part = jnp.zeros((8, 128), F32)
    for h in range(2):
        at = pl.ds(h * HALF, HALF)
        value = blk[at, :]
        hp[at, :] = jnp.dot(value, rrt[...], preferred_element_type=F32).astype(BF16)
        grad_part = grad_part + squares(value)
    starts = ((1 - p) * HALF, p * HALF)
    mids = (mid0, mid1)

    def spread(q, k, away):
        base = starts[0] if away else starts[1]
        return remote(
            pre.at[rows(base + q * PART + rep_at(k) * PIECE, PIECE)],
            mids[q].at[2 * r + p],
            a_s.at[q],
            a_r.at[q],
            rep_at(k),
            pair if away else s,
        )

    for away in (1, 0):
        at = rows(starts[1 - away], HALF)
        value = jnp.dot(lrt[at, :], hp[...], preferred_element_type=F32).astype(BF16)
        pre[at, :] = value
        pre_part = pre_part + squares(value)
    def spread_done(q):
        pieces = mids[q].at[pl.ds(0, 15)]
        return remote(pieces, pieces, a_s.at[q], a_r.at[q], r, pair)

    def spread_all(q):
        for k in range(REP):
            spread(q, k, 1).start()
            if k:
                spread(q, k, 0).start()
        mids[q][2 * r + p] = pre[rows(starts[1] + q * PART + r * PIECE, PIECE), :]

    def tell(buf, me, sems, rep, shard):
        return remote(buf.at[me], buf.at[me], sems.at[0], sems.at[1], rep, shard)

    def told(buf, count, sems):
        others = buf.at[pl.ds(0, count - 1)]
        return remote(others, others, sems.at[0], sems.at[1], r, pair)

    z_sends = [tell(zb, z, z_q, r, z_at(k)) for k in range(1, ZS)]
    x_sends = [tell(xb, x, x_q, r, x_at(k)) for k in range(1, XS)]
    r_sends = [tell(rb, r, r_q, rep_at(k), s) for k in range(1, REP)]

    zb[z, 0:8, :] = grad_part
    zb[z, 8:16, :] = pre_part
    for copy in z_sends:
        copy.start()
    spread_all(0)
    spread_all(1)

    def left_step(m, carry):
        at = rows(m * PART, PART)
        gram = lax.dot_general(blk[at, :], blk[...], (((1,), (1,)), ((), ())), preferred_element_type=F32)
        lst[at, :] = 0.95 * lst[at, :] + 0.05 * gram
        return carry

    lax.fori_loop(0, BLK // PART, left_step, 0)
    put_left = pltpu.make_async_copy(lst, new_left.at[0, 0, 0], o_s.at[0])
    put_left.start()

    def collect(q, k):
        target = rep_at(k)
        return remote(
            sb.at[q, k],
            col.at[rows(q * PART + r * PIECE, PIECE)],
            b_s.at[q],
            b_r.at[q],
            target,
            s,
        )

    def collect_done(q):
        pieces = sb.at[q, pl.ds(1, REP - 1)]
        return remote(pieces, pieces, b_s.at[q], b_r.at[q], r, pair)

    def deal(q):
        spread_done(q).wait_recv()
        for k in range(1, REP):
            target = rep_at(k)
            for n in range(2):
                sb[q, k, :, pl.ds(BLK * n, BLK)] = mids[q][tab[s // 2, 2 * target + n]]
            collect(q, k).start()
        for n in range(2):
            col[rows(q * PART + r * PIECE, PIECE), pl.ds(BLK * n, BLK)] = mids[q][tab[s // 2, 2 * r + n]]

    deal(0)
    told(zb, ZS, z_q).wait_recv()
    xb[x] = jnp.sum(zb[...], axis=0)
    for copy in x_sends:
        copy.start()

    deal(1)
    told(xb, XS, x_q).wait_recv()
    rb[r] = jnp.sum(xb[...], axis=0)
    for copy in r_sends:
        copy.start()
    def right_step(m, carry):
        at = rows(m * PART, PART)
        gram = lax.dot_general(blk[:, at], blk[...], (((0,), (0,)), ((), ())), preferred_element_type=F32)
        rst[at, :] = 0.95 * rst[at, :] + 0.05 * gram
        return carry

    lax.fori_loop(0, BLK // PART, right_step, 0)
    put_right = pltpu.make_async_copy(rst, new_right.at[0, 0, 0], o_s.at[1])
    put_right.start()


    remote(ds, dr, ds_s.at[0], ds_r.at[0], sibling, s).wait_send()
    remote(ys, yr, y_s.at[0], y_r.at[0, 0], sibling, s).wait_send()
    remote(xs, xs, x_s.at[0], x_r.at[0], r, pair).wait_send()
    told(zb, ZS, z_q).wait_send()
    told(xb, XS, x_q).wait_send()
    for q in range(2):
        spread_done(q).wait_send()

    told(rb, REP, r_q).wait_recv()
    totals = jnp.sum(rb[...], axis=0)
    grad_square = jnp.sum(totals[0:8, :], keepdims=True)
    pre_square = jnp.sum(totals[8:16, :], keepdims=True)
    ratio = jnp.sqrt(grad_square + 1e-06) / jnp.sqrt(pre_square + 1e-06)

    for q in range(2):
        collect_done(q).wait_recv()
        at = pl.ds(q * PART, PART)
        out[at, :] = (col[at, :].astype(F32) * ratio).astype(BF16)
        pltpu.make_async_copy(out.at[at], update.at[at], o_s.at[2 + q]).start()

    told(rb, REP, r_q).wait_send()
    for q in range(2):
        collect_done(q).wait_send()
    put_left.wait()
    put_right.wait()
    for q in range(2):
        at = pl.ds(q * PART, PART)
        pltpu.make_async_copy(out.at[at], update.at[at], o_s.at[2 + q]).wait()


def put_out(a, b, c, out_a, out_b, out_c, sems):
    copies = [
        pltpu.make_async_copy(src, dst, sems.at[n]) for n, (src, dst) in enumerate(((c, out_c), (a, out_a), (b, out_b)))
    ]
    for copy in copies:
        copy.start()
    for copy in copies:
        copy.wait()


def shards(gradients, owner_table, left_stats, right_stats, left_root, right_root):
    anywhere = pl.BlockSpec(memory_space=pl.ANY)
    dma = pltpu.SemaphoreType.DMA
    operands = (gradients, owner_table, left_stats, right_stats, left_root, right_root)
    results = pl.pallas_call(
        kernel,
        out_shape=(
            pltpu.VMEM(left_stats.shape, F32),
            pltpu.VMEM(right_stats.shape, F32),
            pltpu.VMEM((HALF, 2 * BLK), BF16),
        ),
        in_specs=[anywhere] * 6,
        out_specs=(anywhere,) * 3,
        scratch_shapes=[
            pltpu.VMEM((16, PART, BLK), BF16),
            pltpu.VMEM((16, PART, BLK), BF16),
            pltpu.SMEM((16, 16), jnp.int32),
            pltpu.SMEM((16,), jnp.int32),
            pltpu.VMEM((8, HALF, BLK), BF16),
            pltpu.VMEM((8, HALF, BLK), BF16),
            pltpu.VMEM((2, 6, PART, BLK), BF16),
            pltpu.VMEM((2, 6, PART, BLK), BF16),
            pltpu.VMEM((2, PART, BLK), BF16),
            pltpu.VMEM((BLK, BLK), BF16),
            pltpu.VMEM((BLK, BLK), F32),
            pltpu.VMEM((BLK, BLK), F32),
            pltpu.VMEM((BLK, BLK), BF16),
            pltpu.VMEM((BLK, BLK), BF16),
            pltpu.VMEM((BLK, BLK), BF16),
            pltpu.VMEM((BLK, BLK), BF16),
            pltpu.VMEM((16, PIECE, BLK), BF16),
            pltpu.VMEM((16, PIECE, BLK), BF16),
            pltpu.VMEM((2, REP, PIECE, 2 * BLK), BF16),
            pltpu.VMEM((HALF, 2 * BLK), BF16),
            pltpu.VMEM((HALF, 2 * BLK), BF16),
            pltpu.VMEM((ZS, 16, 128), F32),
            pltpu.VMEM((XS, 16, 128), F32),
            pltpu.VMEM((REP, 16, 128), F32),
            dma((7,)),
            dma((1,)), dma((9,)),
            dma((1,)), dma((2, 6)),
            dma((1,)), dma((2,)),
            dma((2,)), dma((2,)),
            dma((2,)), dma((2,)),
            dma((2,)), dma((2,)), dma((2,)),
            dma((4,)),
            pltpu.SemaphoreType.REGULAR((3,)),
        ],
        compiler_params=pltpu.CompilerParams(
            collective_id=0, has_side_effects=True, vmem_limit_bytes=40 << 20
        ),
        name="shampoo",
    )(*(pltpu.with_memory_space_constraint(v, pltpu.HBM) for v in operands))
    return pl.pallas_call(
        put_out,
        out_shape=tuple(jax.ShapeDtypeStruct(v.shape, v.dtype) for v in results),
        in_specs=[anywhere] * 3,
        out_specs=(anywhere,) * 3,
        scratch_shapes=[dma((3,))],
        compiler_params=pltpu.CompilerParams(vmem_limit_bytes=4 << 20),
        name="put_out",
    )(*(pltpu.with_memory_space_constraint(v, pltpu.VMEM) for v in results))


def solution(mesh):
    slots = P("rep", "shard", None, None, None)
    return jax.shard_map(
        shards,
        mesh=mesh,
        in_specs=(P("rep", "shard", None), P(), slots, slots, slots, slots),
        out_specs=(slots, slots, P("shard", "rep")),
        check_vma=False,
    )
```
